512 devices in a mesh: row: 32 (over z_lo, y, core), col: 16 (over x, z_hi).
Axes of the slice: x: 4, y: 8, z: 8 (z_hi: 4, z_lo: 2; z = z_hi * 2 + z_lo), core: 2. Of those that a mesh axis runs over, the one named last changes fastest.
Arguments:
- amplitudes: bfloat16 [512, 160, 256], P(('row', 'col')), may hold values from -6 to 6
- tile_edges: int32 [512], P(('row', 'col')), may hold values from 96 to 160
- integrals: bfloat16 [512, 16, 5, 160, 160], P('row', 'col'), may hold values from -0.078125 to 0.078125
- source_rows: int32 [512, 16, 5], P('row', 'col'), may hold values from 0 to 31, as said below
- live_counts: int32 [512, 16], P('row', 'col'), may hold values from 2 to 5
Outputs:
- residual: float32 [512, 160, 256], P(('row', 'col'))
The draws below stay inside these ranges and needn't reach their ends.
Inputs may be any that keep to these rules, and one draw needn't show every extreme that they name: source_rows[a, c, j] differs from a // 16 by at most 3.
All inputs are finite; a program needn't handle non-finite values.
Results may differ from the reference program's by a relative error of at most 0.0003.
Values may be sent and summed in bfloat16 or wider, within the bound.
A program may use at most 64 MiB of HBM per device.

```python
import jax
import jax.numpy as jnp
from jax import lax

E = 160
P_SIZE = 256
BLK = 5
HALF = 3
ROWS = 32
COLS = 16
TILES = 512
EMIN = 96


def draw_source_rows(key, part):
    key = jax.random.fold_in(key, 11)
    tile_row = jnp.arange(TILES) // COLS
    offsets = jax.random.randint(key, (TILES, COLS, BLK), -HALF, HALF + 1)
    offsets = offsets.at[0, 0, 0].set(HALF)
    return jnp.clip(tile_row[:, None, None] + offsets, 0, ROWS - 1).astype(jnp.int32)


def draw_live_counts(key, part):
    key = jax.random.fold_in(key, 12)
    first_key, second_key, third_key = jax.random.split(key, 3)
    density = jax.random.randint(first_key, (ROWS, COLS), 2, BLK + 1)
    raw_counts = jax.random.randint(second_key, (TILES, COLS), 2, BLK + 1)
    tile_row = jnp.arange(TILES) // COLS
    bounded = jnp.minimum(raw_counts, density[tile_row, :])
    where_full = jax.random.randint(third_key, (2,), 0, jnp.array([TILES, COLS]))
    bounded = bounded.at[where_full[0], where_full[1]].set(BLK)
    return bounded.astype(jnp.int32)


def place_ends(values, rng, low, largest):
    place = [jax.random.randint(jax.random.fold_in(rng, axis), (), 0, length) for axis, length in enumerate(values.shape)]
    widest = values.shape.index(max(values.shape))
    next_to = place[:widest] + [(place[widest] + 1) % values.shape[widest]] + place[widest + 1:]
    return values.at[tuple(place)].set(low).at[tuple(next_to)].set(largest)


def shard_levels(rng, dims, pieces, low, largest):
    def one(axis_at, blocks):
        heights = jax.random.uniform(jax.random.fold_in(jax.random.fold_in(rng, 6), axis_at), (blocks,), jnp.float32, low / len(pieces), largest / len(pieces))
        return jnp.repeat(jnp.exp(heights), dims[axis_at] // blocks).reshape((-1,) + (1,) * (len(dims) - axis_at - 1))

    loudness = one(*pieces[0])
    for cut in pieces[1:]:
        loudness = loudness * one(*cut)
    return loudness


def bell_draw(own_key, dims, width, most, cuts=(), dtype=jnp.bfloat16):
    gain = shard_levels(own_key, dims, cuts, -0.22, 0.18) if cuts else 1.0
    entries = jax.random.normal(own_key, dims, jnp.float32) * width * gain
    return jnp.minimum(jnp.maximum(entries, -most), most).astype(dtype)


def setup_inputs(seed: int = 0) -> dict:
    seeds = jax.random.split(jax.random.key(seed), 6)
    return {
        "amplitudes": bell_draw(seeds[0], (TILES, E, P_SIZE), 1.0, 6.0, ((0, 512),)),
        "tile_edges": place_ends(jax.random.randint(seeds[1], (TILES,), EMIN, E + 1), jax.random.fold_in(seeds[1], 1), EMIN, E).astype(jnp.int32),
        "integrals": bell_draw(seeds[2], (TILES, COLS, BLK, E, E), (E * BLK * COLS // 2) ** -0.5, 0.078125, ((0, 32), (1, 16))),
        "source_rows": draw_source_rows(jax.random.fold_in(seeds[5], 71), 0),
        "live_counts": draw_live_counts(jax.random.fold_in(seeds[5], 71), 0),
    }


def reference(amplitudes, tile_edges, integrals, source_rows, live_counts):
    positions = jnp.arange(E)
    masked = jnp.where(positions[None, :, None] < tile_edges[:, None, None], amplitudes, jnp.zeros_like(amplitudes))
    columns = jnp.arange(COLS)
    slots = jnp.arange(BLK)

    def one_tile(inputs):
        weights, rows_from, alive_count, edge = inputs
        tiles = (rows_from * COLS + columns[:, None]).astype(jnp.int32)
        picked = jnp.take(masked, tiles, axis=0).astype(jnp.float32)
        alive = slots[None, :] < alive_count[:, None]
        picked = jnp.where(alive[:, :, None, None], picked, jnp.zeros_like(picked))
        terms = jnp.einsum('cbxy,cbyp->cxp', weights.astype(jnp.float32), picked)
        total = jnp.sum(terms, axis=0)
        return jnp.where(positions[:, None] < edge, total, jnp.zeros_like(total))

    return lax.map(one_tile, (integrals, source_rows, live_counts, tile_edges))
```

```python
import functools

import jax
import jax.numpy as jnp
from jax import lax
from jax.experimental import pallas as pl
from jax.experimental.pallas import tpu as pltpu
from jax.sharding import PartitionSpec as P

HALF = 3
SIDE = 4
DEAD = 2 * HALF + 1
EXP_ROWS = 16
TINY = 2.0**-110
LANES = 128

WAY = {
    (0, 2, 0): "up",
    (0, 2, 1): "down",
    (2, 0, 0): "left",
    (2, 0, 1): "right",
    (2, 1, 0): "up",
    (2, 1, 1): "up",
    (2, 2, 0): "left",
    (2, 2, 1): "right_2",
    (2, 3, 0): "down",
    (2, 3, 1): "down",
}

SEND, PASS, ALL = 3, 4, 5
ORDER = (
    (1, 1, 0), (1, 1, 0, SEND), (2, 2, 0), (2, 2, 0, SEND), (1, 2, 0), (PASS,), (1, 2, 0, SEND), (0, 0, 0),
    (2, 3, 0), (2, 3, 0, SEND), (0, 2, 0), (ALL,), (2, 2, 1), (2, 2, 1, SEND), (3, 2, 2), (3, 2, 1, SEND),
    (2, 1, 2), (2, 1, 1, SEND), (3, 3, 2), (1, 2, 1), (1, 2, 1, SEND), (3, 2, 0, SEND), (2, 1, 0, SEND),
    (3, 3, 0, SEND), (2, 3, 1), (2, 3, 1, SEND), (1, 1, 1), (1, 1, 1, SEND), (1, 3, 2), (1, 3, 0, SEND),
    (3, 1, 2), (3, 1, 1, SEND), (3, 1, 0, SEND), (0, 1, 2), (0, 2, 1), (0, 0, 1), (3, 3, 1, SEND), (2, 0, 2),
    (0, 2, 0, SEND), (0, 2, 1, SEND), (1, 0, 2), (1, 3, 1, SEND), (3, 0, 2), (3, 0, 1, SEND), (0, 3, 2),
    (1, 0, 0, SEND), (2, 0, 1, SEND), (0, 1, 1, SEND), (0, 3, 0, SEND), (2, 0, 0, SEND), (0, 1, 0, SEND),
    (0, 3, 1, SEND), (3, 0, 0, SEND), (1, 0, 1, SEND),
)


MOVES = {"right": (1, 0), "left": (-1, 0), "up": (0, 1), "down": (0, -1), "right_2": (2, 0), "up_2": (0, 2)}


def way(dx, dz, side):
    if (dx, dz, side) in WAY:
        return WAY[dx, dz, side]
    if dx:
        return "right" if dx == 1 else "left"
    return "up" if dz == 1 else "down"


def onward(dx, dz, side):
    by_x, by_z = MOVES[way(dx, dz, side)]
    return (dx - by_x) % SIDE, (dz - by_z) % SIDE, side


NODES = [(dx, dz, side) for dx in range(SIDE) for dz in range(SIDE) for side in (0, 1) if dx or dz]


def arriving(node):
    return [other for other in NODES if onward(*other) == node]


def kernel(
    size, rows,
    amp_ref, edge_ref, src_ref, live_ref, weight_ref, out_ref,
    amp, src, live, weight, window_0, window_1, part, outbox, inbox,
    load_sem, row_send, row_recv, send_sem, recv_sem,
):
    window = (window_0, window_1)
    slots = weight_ref.shape[2]
    edge_len = amp_ref.shape[1]
    me_row = lax.axis_index("row")
    me_col = lax.axis_index("col")
    me_x = me_col // SIDE
    me_z = me_col % SIDE

    def row_at(by):
        return {"row": lax.rem(me_row + by + rows, rows)}

    def col_at(by_x, by_z):
        return {"col": lax.rem(me_x + by_x + SIDE, SIDE) * SIDE + lax.rem(me_z + by_z + SIDE, SIDE)}

    used = {way(*node) for node in NODES}
    neighbours = {name: col_at(*by) for name, by in MOVES.items() if name in used}

    amp_copy = pltpu.make_async_copy(amp_ref.at[0], amp, load_sem.at[0])
    amp_copy.start()
    barrier = pltpu.get_barrier_semaphore()
    core = lax.rem(me_row, 2)
    beyond = 6 * core - HALF
    sibling = 1 - 2 * core
    chip, last_chip = me_row // 2, rows // 2 - 1
    has = {2: chip < last_chip, -2: chip > 0}
    has_beyond = jnp.logical_and(me_row + beyond >= 0, me_row + beyond < rows)

    def where(condition, act):
        if condition is None:
            act()
        else:
            pl.when(condition)(act)

    def greet(partner):
        pl.semaphore_signal(barrier, inc=1, device_id=partner, device_id_type=pl.DeviceIdType.MESH)

    for partner in [row_at(sibling), *neighbours.values()]:
        greet(partner)
    row_partners = [(2, has[2]), (-2, has[-2]), (beyond, has_beyond)]
    for by, condition in row_partners:
        where(condition, functools.partial(greet, row_at(by)))
    expected = 1 + len(neighbours) + sum(condition.astype(jnp.int32) for _, condition in row_partners)
    loads = [
        pltpu.make_async_copy(src_ref, src, load_sem.at[1]),
        pltpu.make_async_copy(live_ref, live, load_sem.at[2]),
        pltpu.make_async_copy(weight_ref.at[:, 0], weight, load_sem.at[3]),
    ]
    edge = edge_ref[0]
    kept = lax.broadcasted_iota(jnp.int32, (edge_len, LANES), 0) < edge
    for side in (0, 1):
        window[side][DEAD] = jnp.zeros((edge_len, LANES), amp.dtype)
    amp_copy.wait()
    for side in (0, 1):
        columns = amp[:, side * LANES:(side + 1) * LANES].astype(jnp.float32)
        window[side][HALF] = jnp.where(kept, columns, 0.0).astype(amp.dtype)
    pl.semaphore_wait(barrier, expected)

    def row_copy(side, place, source, target, by):
        return pltpu.make_async_remote_copy(
            src_ref=window[side].at[source],
            dst_ref=window[side].at[target],
            send_sem=row_send.at[6 * side + place],
            recv_sem=row_recv.at[6 * side + place],
            device_id=row_at(by),
            device_id_type=pl.DeviceIdType.MESH,
        )

    own = [
        [
            (row_copy(side, 0, HALF, HALF - 2, 2), has[2], has[-2]),
            (row_copy(side, 1, HALF, HALF + 2, -2), has[-2], has[2]),
            (row_copy(side, 2, HALF, HALF - sibling, sibling), None, None),
            (row_copy(side, 3, HALF, HALF - beyond, beyond), has_beyond, has_beyond),
        ]
        for side in (0, 1)
    ]
    passed_on = [
        [
            (row_copy(side, 4, HALF - 2, HALF - 2 - sibling, sibling), has[-2], has[-2]),
            (row_copy(side, 5, HALF + 2, HALF + 2 - sibling, sibling), has[2], has[2]),
        ]
        for side in (0, 1)
    ]
    for copy, sends, _ in own[0] + own[1]:
        where(sends, copy.start)
    for copy in loads:
        copy.start()

    def pass_on(side):
        for (arrived, _, receives), (copy, _, _) in zip(own[side], passed_on[side]):
            def forward(arrived=arrived, copy=copy):
                arrived.wait_recv()
                copy.start()

            where(receives, forward)

    def wait_window(side):
        for copy, _, receives in own[side][2:] + passed_on[side]:
            where(receives, copy.wait_recv)

    def place_of(node):
        return (node[0] * SIDE + node[1] - 1) * 2 + node[2]

    def message(node):
        place = place_of(node)
        return pltpu.make_async_remote_copy(
            src_ref=outbox.at[place],
            dst_ref=inbox.at[place],
            send_sem=send_sem.at[place],
            recv_sem=recv_sem.at[place],
            device_id=neighbours[way(*node)],
            device_id_type=pl.DeviceIdType.MESH,
        )

    messages = {node: message(node) for node in NODES}

    def multiply(dx, dz, sides):
        tile = lax.rem(me_x + dx, SIDE) * SIDE + lax.rem(me_z + dz, SIDE)
        count = live[0, tile]
        total = None
        for slot in range(slots):
            place = jnp.where(slot < count, src[slot, 0, tile] - me_row + HALF, DEAD)
            columns = [window[side][place] for side in sides]
            columns = columns[0] if len(columns) == 1 else jnp.concatenate(columns, axis=1)
            term = jnp.dot(weight[tile, slot], columns, preferred_element_type=jnp.float32)
            total = term if total is None else total + term
        for place, side in enumerate(sides):
            part[side, dx * SIDE + dz] = total[:, place * LANES:(place + 1) * LANES]

    def summed(node):
        value = part[node[2], node[0] * SIDE + node[1]]
        for other in arriving(node):
            messages[other].wait_recv()
            place = place_of(other)
            exponent = inbox[place, edge_len:].astype(jnp.float32)[:1]
            value += inbox[place, :edge_len].astype(jnp.float32) * jnp.exp2(exponent)
        return value

    def send(node):
        value = summed(node)
        place = place_of(node)
        most = jnp.maximum(jnp.max(jnp.abs(value), axis=0, keepdims=True), TINY)
        exponent = jnp.ceil(jnp.log2(most * 1.0001)) - 15.0
        outbox[place, :edge_len] = jnp.round(value * jnp.exp2(-exponent)).astype(jnp.int16)
        outbox[place, edge_len:] = jnp.broadcast_to(exponent, (EXP_ROWS, LANES)).astype(jnp.int16)
        messages[node].start()

    pass_on(0)
    for copy in loads:
        copy.wait()
    wait_window(0)
    for step in ORDER:
        kind = step[-1]
        if kind == SEND:
            send(step[:3])
        elif kind == PASS:
            pass_on(1)
        elif kind == ALL:
            wait_window(1)
        else:
            multiply(*step[:2], (0, 1) if kind == 2 else (kind,))

    for side in (0, 1):
        out_ref[0, :, side * LANES:(side + 1) * LANES] = jnp.where(kept, summed((0, 0, side)), 0.0)
    for copy, sends, _ in own[0] + own[1] + passed_on[0] + passed_on[1]:
        where(sends, copy.wait_send)
    for copy in messages.values():
        copy.wait_send()


def per_device(rows, amplitudes, tile_edges, integrals, source_rows, live_counts):
    size, _, slots, edge_len, _ = integrals.shape
    width = amplitudes.shape[2]
    any_space = pl.BlockSpec(memory_space=pl.ANY)
    in_hbm = functools.partial(pltpu.with_memory_space_constraint, memory_space=pltpu.HBM)
    return pl.pallas_call(
        functools.partial(kernel, size, rows),
        out_shape=pltpu.VMEM((1, edge_len, width), jnp.float32),
        in_specs=[any_space, pl.BlockSpec(memory_space=pltpu.SMEM), any_space, any_space, any_space],
        out_specs=pl.BlockSpec(memory_space=pltpu.VMEM),
        scratch_shapes=[
            pltpu.VMEM((edge_len, width), amplitudes.dtype),
            pltpu.SMEM((slots, 1, size), jnp.int32),
            pltpu.SMEM((1, size), jnp.int32),
            pltpu.VMEM((size, slots, edge_len, edge_len), integrals.dtype),
            pltpu.VMEM((2 * HALF + 2, edge_len, LANES), amplitudes.dtype),
            pltpu.VMEM((2 * HALF + 2, edge_len, LANES), amplitudes.dtype),
            pltpu.VMEM((2, size, edge_len, LANES), jnp.float32),
            pltpu.VMEM((len(NODES), edge_len + EXP_ROWS, LANES), jnp.int16),
            pltpu.VMEM((len(NODES), edge_len + EXP_ROWS, LANES), jnp.int16),
            pltpu.SemaphoreType.DMA((4,)),
            pltpu.SemaphoreType.DMA((12,)),
            pltpu.SemaphoreType.DMA((12,)),
            pltpu.SemaphoreType.DMA((len(NODES),)),
            pltpu.SemaphoreType.DMA((len(NODES),)),
        ],
        compiler_params=pltpu.CompilerParams(
            collective_id=0, has_side_effects=True, vmem_limit_bytes=60 * 1024 * 1024
        ),
        cost_estimate=pl.CostEstimate(
            flops=2 * size * slots * edge_len * edge_len * width,
            bytes_accessed=2 * size * slots * edge_len * edge_len,
            transcendentals=0,
        ),
    )(
        in_hbm(amplitudes),
        tile_edges,
        in_hbm(source_rows.transpose(2, 1, 0)),
        in_hbm(live_counts.transpose(1, 0)),
        in_hbm(integrals),
    )


def solution(mesh):
    return jax.shard_map(
        functools.partial(per_device, mesh.shape["row"]),
        mesh=mesh,
        in_specs=(
            P(("row", "col"), None, None),
            P(("row", "col")),
            P("row", "col", None, None, None),
            P("row", "col", None),
            P("row", "col"),
        ),
        out_specs=P(("row", "col"), None, None),
        check_vma=False,
    )
```

```python
import functools

import jax
import jax.numpy as jnp
from jax import lax
from jax.experimental import pallas as pl
from jax.experimental.pallas import tpu as pltpu
from jax.sharding import PartitionSpec as P

HALF = 3
SIDE = 4
DEAD = 2 * HALF + 1
EXP_ROWS = 16
TINY = 2.0**-110
LANES = 128

WAY = {
    (0, 2, 0): "up",
    (0, 2, 1): "up_2",
    (2, 0, 0): "left",
    (2, 0, 1): "right",
    (2, 1, 0): "up",
    (2, 1, 1): "up",
    (2, 2, 0): "left",
    (2, 2, 1): "right_2",
    (2, 3, 0): "down",
    (2, 3, 1): "down",
}

SEND, PASS, ALL = 3, 4, 5
ORDER = (
    (2, 2, 0), (2, 2, 0, SEND), (1, 2, 0), (1, 2, 0, SEND), (PASS,), (2, 3, 0), (2, 3, 0, SEND), (1, 3, 0),
    (1, 3, 0, SEND), (3, 3, 0), (3, 3, 0, SEND), (ALL,), (2, 2, 1), (2, 2, 1, SEND), (2, 3, 1), (2, 1, 2),
    (2, 1, 1, SEND), (3, 2, 2), (2, 3, 1, SEND), (3, 2, 0, SEND), (1, 2, 1), (1, 2, 1, SEND), (3, 2, 1, SEND),
    (3, 1, 2), (3, 1, 1, SEND), (2, 1, 0, SEND), (0, 3, 2), (0, 3, 0, SEND), (1, 1, 2), (1, 1, 1, SEND),
    (1, 1, 0, SEND), (1, 3, 1), (1, 3, 1, SEND), (0, 2, 2), (3, 3, 1), (0, 2, 0, SEND), (3, 3, 1, SEND),
    (0, 1, 2), (3, 1, 0, SEND), (0, 2, 1, SEND), (0, 0, 2), (2, 0, 2), (2, 0, 1, SEND), (0, 1, 1, SEND),
    (2, 0, 0, SEND), (3, 0, 2), (3, 0, 1, SEND), (1, 0, 2), (1, 0, 0, SEND), (0, 3, 1, SEND), (0, 1, 0, SEND),
    (1, 0, 1, SEND), (3, 0, 0, SEND),
)


MOVES = {"right": (1, 0), "left": (-1, 0), "up": (0, 1), "down": (0, -1), "right_2": (2, 0), "up_2": (0, 2)}


def way(dx, dz, side):
    if (dx, dz, side) in WAY:
        return WAY[dx, dz, side]
    if dx:
        return "right" if dx == 1 else "left"
    return "up" if dz == 1 else "down"


def onward(dx, dz, side):
    by_x, by_z = MOVES[way(dx, dz, side)]
    return (dx - by_x) % SIDE, (dz - by_z) % SIDE, side


NODES = [(dx, dz, side) for dx in range(SIDE) for dz in range(SIDE) for side in (0, 1) if dx or dz]


def arriving(node):
    return [other for other in NODES if onward(*other) == node]


def kernel(
    size, rows,
    amp_ref, edge_ref, src_ref, live_ref, weight_ref, out_ref,
    amp, src, live, weight, window_0, window_1, part, outbox, inbox,
    load_sem, row_send, row_recv, send_sem, recv_sem,
):
    window = (window_0, window_1)
    slots = weight_ref.shape[2]
    edge_len = amp_ref.shape[1]
    me_row = lax.axis_index("row")
    me_col = lax.axis_index("col")
    me_x = me_col // SIDE
    me_z = me_col % SIDE

    def row_at(by):
        return {"row": lax.rem(me_row + by + rows, rows)}

    def col_at(by_x, by_z):
        return {"col": lax.rem(me_x + by_x + SIDE, SIDE) * SIDE + lax.rem(me_z + by_z + SIDE, SIDE)}

    used = {way(*node) for node in NODES}
    neighbours = {name: col_at(*by) for name, by in MOVES.items() if name in used}

    amp_copy = pltpu.make_async_copy(amp_ref.at[0], amp, load_sem.at[0])
    amp_copy.start()
    barrier = pltpu.get_barrier_semaphore()
    core = lax.rem(me_row, 2)
    beyond = 6 * core - HALF
    sibling = 1 - 2 * core
    chip, last_chip = me_row // 2, rows // 2 - 1
    has = {2: chip < last_chip, -2: chip > 0}
    has_beyond = jnp.logical_and(me_row + beyond >= 0, me_row + beyond < rows)

    def where(condition, act):
        if condition is None:
            act()
        else:
            pl.when(condition)(act)

    def greet(partner):
        pl.semaphore_signal(barrier, inc=1, device_id=partner, device_id_type=pl.DeviceIdType.MESH)

    row_partners = [(2, has[2]), (-2, has[-2]), (beyond, has_beyond)]
    for by, condition in row_partners:
        where(condition, functools.partial(greet, row_at(by)))
    for partner in [row_at(sibling), *neighbours.values()]:
        greet(partner)
    expected = 1 + len(neighbours) + sum(condition.astype(jnp.int32) for _, condition in row_partners)
    loads = [
        pltpu.make_async_copy(src_ref, src, load_sem.at[1]),
        pltpu.make_async_copy(live_ref, live, load_sem.at[2]),
        pltpu.make_async_copy(weight_ref.at[:, 0], weight, load_sem.at[3]),
    ]
    edge = edge_ref[0]
    kept = lax.broadcasted_iota(jnp.int32, (edge_len, LANES), 0) < edge
    for side in (0, 1):
        window[side][DEAD] = jnp.zeros((edge_len, LANES), amp.dtype)
    amp_copy.wait()
    for side in (0, 1):
        columns = amp[:, side * LANES:(side + 1) * LANES].astype(jnp.float32)
        window[side][HALF] = jnp.where(kept, columns, 0.0).astype(amp.dtype)
    pl.semaphore_wait(barrier, expected)

    def row_copy(side, place, source, target, by):
        return pltpu.make_async_remote_copy(
            src_ref=window[side].at[source],
            dst_ref=window[side].at[target],
            send_sem=row_send.at[6 * side + place],
            recv_sem=row_recv.at[6 * side + place],
            device_id=row_at(by),
            device_id_type=pl.DeviceIdType.MESH,
        )

    own = [
        [
            (row_copy(side, 0, HALF, HALF - 2, 2), has[2], has[-2]),
            (row_copy(side, 1, HALF, HALF + 2, -2), has[-2], has[2]),
            (row_copy(side, 2, HALF, HALF - sibling, sibling), None, None),
            (row_copy(side, 3, HALF, HALF - beyond, beyond), has_beyond, has_beyond),
        ]
        for side in (0, 1)
    ]
    passed_on = [
        [
            (row_copy(side, 4, HALF - 2, HALF - 2 - sibling, sibling), has[-2], has[-2]),
            (row_copy(side, 5, HALF + 2, HALF + 2 - sibling, sibling), has[2], has[2]),
        ]
        for side in (0, 1)
    ]
    for copy, sends, _ in own[0] + own[1]:
        where(sends, copy.start)
    for copy in loads:
        copy.start()

    def pass_on(side):
        for (arrived, _, receives), (copy, _, _) in zip(own[side], passed_on[side]):
            def forward(arrived=arrived, copy=copy):
                arrived.wait_recv()
                copy.start()

            where(receives, forward)

    def wait_window(side):
        for copy, _, receives in own[side][2:] + passed_on[side]:
            where(receives, copy.wait_recv)

    def place_of(node):
        return (node[0] * SIDE + node[1] - 1) * 2 + node[2]

    def message(node):
        place = place_of(node)
        return pltpu.make_async_remote_copy(
            src_ref=outbox.at[place],
            dst_ref=inbox.at[place],
            send_sem=send_sem.at[place],
            recv_sem=recv_sem.at[place],
            device_id=neighbours[way(*node)],
            device_id_type=pl.DeviceIdType.MESH,
        )

    messages = {node: message(node) for node in NODES}

    def multiply(dx, dz, sides):
        tile = lax.rem(me_x + dx, SIDE) * SIDE + lax.rem(me_z + dz, SIDE)
        count = live[0, tile]
        total = None
        for slot in range(slots):
            place = jnp.where(slot < count, src[slot, 0, tile] - me_row + HALF, DEAD)
            columns = [window[side][place] for side in sides]
            columns = columns[0] if len(columns) == 1 else jnp.concatenate(columns, axis=1)
            term = jnp.dot(weight[tile, slot], columns, preferred_element_type=jnp.float32)
            total = term if total is None else total + term
        for place, side in enumerate(sides):
            part[side, dx * SIDE + dz] = total[:, place * LANES:(place + 1) * LANES]

    def summed(node):
        value = part[node[2], node[0] * SIDE + node[1]]
        for other in arriving(node):
            messages[other].wait_recv()
            place = place_of(other)
            exponent = inbox[place, edge_len:].astype(jnp.float32)[:1]
            value += inbox[place, :edge_len].astype(jnp.float32) * jnp.exp2(exponent)
        return value

    def send(node):
        value = summed(node)
        place = place_of(node)
        most = jnp.maximum(jnp.max(jnp.abs(value), axis=0, keepdims=True), TINY)
        exponent = jnp.ceil(jnp.log2(most * 1.0001)) - 15.0
        outbox[place, :edge_len] = jnp.round(value * jnp.exp2(-exponent)).astype(jnp.int16)
        outbox[place, edge_len:] = jnp.broadcast_to(exponent, (EXP_ROWS, LANES)).astype(jnp.int16)
        messages[node].start()

    pass_on(0)
    for copy in loads:
        copy.wait()
    wait_window(0)
    for step in ORDER:
        kind = step[-1]
        if kind == SEND:
            send(step[:3])
        elif kind == PASS:
            pass_on(1)
        elif kind == ALL:
            wait_window(1)
        else:
            multiply(*step[:2], (0, 1) if kind == 2 else (kind,))

    for side in (0, 1):
        out_ref[0, :, side * LANES:(side + 1) * LANES] = jnp.where(kept, summed((0, 0, side)), 0.0)
    for copy, sends, _ in own[0] + own[1] + passed_on[0] + passed_on[1]:
        where(sends, copy.wait_send)
    for copy in messages.values():
        copy.wait_send()


def per_device(rows, amplitudes, tile_edges, integrals, source_rows, live_counts):
    size, _, slots, edge_len, _ = integrals.shape
    width = amplitudes.shape[2]
    any_space = pl.BlockSpec(memory_space=pl.ANY)
    in_hbm = functools.partial(pltpu.with_memory_space_constraint, memory_space=pltpu.HBM)
    return pl.pallas_call(
        functools.partial(kernel, size, rows),
        out_shape=pltpu.VMEM((1, edge_len, width), jnp.float32),
        in_specs=[any_space, pl.BlockSpec(memory_space=pltpu.SMEM), any_space, any_space, any_space],
        out_specs=pl.BlockSpec(memory_space=pltpu.VMEM),
        scratch_shapes=[
            pltpu.VMEM((edge_len, width), amplitudes.dtype),
            pltpu.SMEM((slots, 1, size), jnp.int32),
            pltpu.SMEM((1, size), jnp.int32),
            pltpu.VMEM((size, slots, edge_len, edge_len), integrals.dtype),
            pltpu.VMEM((2 * HALF + 2, edge_len, LANES), amplitudes.dtype),
            pltpu.VMEM((2 * HALF + 2, edge_len, LANES), amplitudes.dtype),
            pltpu.VMEM((2, size, edge_len, LANES), jnp.float32),
            pltpu.VMEM((len(NODES), edge_len + EXP_ROWS, LANES), jnp.int16),
            pltpu.VMEM((len(NODES), edge_len + EXP_ROWS, LANES), jnp.int16),
            pltpu.SemaphoreType.DMA((4,)),
            pltpu.SemaphoreType.DMA((12,)),
            pltpu.SemaphoreType.DMA((12,)),
            pltpu.SemaphoreType.DMA((len(NODES),)),
            pltpu.SemaphoreType.DMA((len(NODES),)),
        ],
        compiler_params=pltpu.CompilerParams(
            collective_id=0, has_side_effects=True, vmem_limit_bytes=60 * 1024 * 1024
        ),
        cost_estimate=pl.CostEstimate(
            flops=2 * size * slots * edge_len * edge_len * width,
            bytes_accessed=2 * size * slots * edge_len * edge_len,
            transcendentals=0,
        ),
    )(
        in_hbm(amplitudes),
        tile_edges,
        in_hbm(source_rows.transpose(2, 1, 0)),
        in_hbm(live_counts.transpose(1, 0)),
        in_hbm(integrals),
    )


def solution(mesh):
    return jax.shard_map(
        functools.partial(per_device, mesh.shape["row"]),
        mesh=mesh,
        in_specs=(
            P(("row", "col"), None, None),
            P(("row", "col")),
            P("row", "col", None, None, None),
            P("row", "col", None),
            P("row", "col"),
        ),
        out_specs=P(("row", "col"), None, None),
        check_vma=False,
    )
```
